512 devices in a mesh: ctx: 16 (over y, x), exp: 32 (over z, core).
Axes of the slice: x: 4, y: 4, z: 16, core: 2. Of those that a mesh axis runs over, the one named last changes fastest.
Arguments:
- query_heads: bfloat16 [16384, 32, 128], P('ctx', 'exp'), may hold values from -0.59765625 to 0.59765625
- key_heads: bfloat16 [16384, 32, 128], P('ctx', 'exp'), may hold values from -0.59765625 to 0.59765625
- value_heads: bfloat16 [16384, 32, 128], P('ctx', 'exp'), may hold values from -6 to 6
- out_grad: bfloat16 [16384, 32, 128], P('ctx', 'exp'), may hold values from -0.29882812 to 0.29882812
- log_decay: bfloat16 [16384, 32, 128], P('ctx', 'exp'), may hold values from -1 to 0, as said below
- start_state: float32 [16, 32, 128, 128], P('ctx', 'exp'), may hold values from -24 to 24
- layer_grad: bfloat16 [16384, 2304], P(('ctx', 'exp')), may hold values from -6 to 6
- gate_weights: float32 [16384, 8], P(('ctx', 'exp')), may hold values from 0.1 to 1
- routes: int32 [16384, 8], P(('ctx', 'exp')), may hold values from 0 to 31, all different within a row; in each aligned block of 32 rows (0 to 31, 32 to 63, ...) at most 16 rows name the same one
- expert_down: bfloat16 [32, 512, 2304], P('exp'), may hold values from -0.125 to 0.125
Outputs:
- query_grad: bfloat16 [16384, 32, 128], P('ctx', 'exp')
- key_grad: bfloat16 [16384, 32, 128], P('ctx', 'exp')
- value_grad: bfloat16 [16384, 32, 128], P('ctx', 'exp')
- hidden_grad: bfloat16 [16, 32, 32, 16, 512], P('ctx', None, 'exp')
The draws below stay inside these ranges and needn't reach their ends.
Inputs may be any that keep to these rules, and one draw needn't show every extreme that they name: `routes`: each row names 8 different experts. Within the 32 rows of one device no expert is named by more than 16 rows, a bound that some block reaches. `log_decay`: every entry is at most zero.
All inputs are finite; a program needn't handle non-finite values.
Results may differ from the reference program's by a relative error of at most 0.0049.
Values may be sent and summed in bfloat16 or wider, within the bound.
No kernel may reach another device: no remote copies, remote signals or barrier semaphores. Data moves between devices by JAX's collectives and lax.ppermute only.
A program may use at most 64 MiB of HBM per device.

```python
import math
import jax
import jax.numpy as jnp
import numpy as np
from jax import lax

D = 2304
KD = 128
VD = 128
TOP = 8
FW = 512
EXPERTS = 32
ROWS_DEV = 32
HEADS = 32
MOST = 16
TOK_CTX = 1024
STREAM_POSITIONS = 16384
GROUPS = 16
SOURCES = 32


def draw_log_decay(key, part):
    key = jax.random.fold_in(key, 11)
    addressing_array = jax.random.split(key, 10)
    slow_share = 0.5
    chooser = jax.random.uniform(addressing_array[0], (HEADS, KD))
    slow_rate = jnp.exp(jax.random.uniform(addressing_array[1], (HEADS, KD), minval=math.log(0.05), maxval=math.log(0.5))) / STREAM_POSITIONS
    fast_rate = jnp.exp(jax.random.uniform(addressing_array[2], (HEADS, KD), minval=math.log(1.0 / 50.0), maxval=math.log(1.0 / 25.0)))
    arriving_rate_count = jnp.where(chooser < slow_share, slow_rate, fast_rate)
    segments = (STREAM_POSITIONS + 63) // 64
    segment_factor = jnp.exp(jax.random.uniform(addressing_array[3], (segments, HEADS, 1), minval=-0.7, maxval=0.7))
    forgetting_multiplier = jnp.repeat(segment_factor, 64, axis=0)[:STREAM_POSITIONS]
    per_position_forgetting = jnp.exp(jax.random.uniform(addressing_array[4], (STREAM_POSITIONS, HEADS, KD), minval=-0.35, maxval=0.35))
    cluster_delivered = jax.random.bernoulli(addressing_array[5], 3.0 / STREAM_POSITIONS, (STREAM_POSITIONS, 1, 1))
    cluster_extent = jax.random.uniform(addressing_array[6], (STREAM_POSITIONS, 1, 1), minval=math.log(0.5), maxval=math.log(0.8))
    content_array = -arriving_rate_count[None, :, :] * forgetting_multiplier * per_position_forgetting + jnp.where(cluster_delivered, cluster_extent, 0.0)
    stretch_length = min(384, STREAM_POSITIONS // 4)
    stretch_start = jax.random.randint(addressing_array[7], (1, HEADS, 1), 0, STREAM_POSITIONS - stretch_length + 1)
    positions = jnp.arange(STREAM_POSITIONS, dtype=jnp.int32)[:, None, None]
    within_stretch = (positions >= stretch_start) & (positions < stretch_start + stretch_length)
    stretch_channel = jax.random.uniform(addressing_array[8], (1, HEADS, KD)) < 0.0625
    steep_values = jax.random.uniform(addressing_array[9], (STREAM_POSITIONS, HEADS, KD), minval=-1.0, maxval=-0.6)
    content_array = jnp.where(within_stretch & stretch_channel, steep_values, content_array)
    return content_array.astype(jnp.float32).astype(jnp.bfloat16)


def block_levels(stream_key, extent, pieces, least, high):
    def one(dim, blocks):
        steps = jax.random.uniform(jax.random.fold_in(jax.random.fold_in(stream_key, 6), dim), (blocks,), jnp.float32, least / len(pieces), high / len(pieces))
        return jnp.repeat(jnp.exp(steps), extent[dim] // blocks).reshape((-1,) + (1,) * (len(extent) - dim - 1))

    level = one(*pieces[0])
    for cut in pieces[1:]:
        level = level * one(*cut)
    return level


def shared_out(rng, own, number, rows, amount, top, most, slope):
    sequence = jax.random.permutation(rng, amount)
    packed, usual = portions_of(amount, rows * top, most, slope, True), portions_of(amount, rows * top, most, slope, False)
    places = jnp.arange(amount)

    def named(lengths, turn):
        used = int((lengths > 0).sum())
        fixed = max(1, used // 4)
        moved = fixed + (places - fixed + turn * (used - fixed)) % max(1, amount - fixed)
        return jnp.zeros((amount,), jnp.int32).at[sequence[jnp.where(places < fixed, places, moved)]].set(jnp.asarray(lengths, jnp.int32))

    lengths = jnp.where(number % 4 == 0, named(packed, number // 4), named(usual, number - number // 4 - 1))
    mixed = jax.random.permutation(jax.random.fold_in(own, 3), amount)
    giver, taker = mixed[0:amount // 2 * 2:2], mixed[1:amount // 2 * 2:2]
    margin = jnp.minimum(lengths[giver] - 1, most - lengths[taker]) // 2
    margin = jnp.where((giver == sequence[0]) | (taker == sequence[0]) | (lengths[taker] == 0), 0, jnp.maximum(margin, 0))
    moved = jax.random.randint(jax.random.fold_in(own, 4), (amount // 2,), 0, 1 << 20) % (margin + 1)
    lengths = lengths.at[giver].add(-moved).at[taker].add(moved)
    items = jnp.searchsorted(jnp.cumsum(lengths), jnp.arange(rows * top), side="right").astype(jnp.int32)
    table = items.reshape(top, rows).T
    table = table[jax.random.permutation(jax.random.fold_in(own, 1), rows)]
    turn = jax.random.randint(jax.random.fold_in(own, 2), (rows, 1), 0, top)
    return jnp.take_along_axis(table, (jnp.arange(top)[None, :] + turn) % top, axis=1)


def portions_of(number_of, total, limit, slope, full):
    weights = [(1 << 20) // math.isqrt(grade ** slope) + 1 for grade in range(1, number_of + 1)]
    largest = limit if full else min(limit, max(-(-total // number_of), total * weights[0] // sum(weights)))
    least = 1 if total - largest >= number_of - 1 else 0
    holding, rest = [largest] + [least] * (number_of - 1), total - largest - least * (number_of - 1)
    while rest > 0:
        candidates = [i for i in range(1, number_of) if holding[i] < largest] or [i for i in range(1, number_of) if holding[i] < limit]
        mass, left = sum([weights[i] for i in candidates]), rest
        for i in candidates:
            extra = min(limit - holding[i], max(1, left * weights[i] // mass), rest)
            holding[i] = holding[i] + extra
            rest = rest - extra
    return np.array(holding)


def gaussian(key, dims, scale, most, pieces=(), kind=jnp.bfloat16):
    result = jax.random.normal(key, dims, jnp.float32) * scale
    if len(pieces) > 0:
        result = block_levels(key, dims, pieces, -0.22, 0.18) * result
    return jnp.clip(result, min=-most, max=most).astype(kind)


def setup_inputs(seed: int = 0) -> dict:
    key_of = jax.random.split(jax.random.key(seed), 11)
    query_heads = gaussian(key_of[0], (STREAM_POSITIONS, HEADS, KD), 0.088, 0.59765625, ((0, 16), (1, 32)))
    key_heads = gaussian(key_of[1], (STREAM_POSITIONS, HEADS, KD), 0.088, 0.59765625, ((0, 16), (1, 32)))
    value_heads = gaussian(key_of[2], (STREAM_POSITIONS, HEADS, VD), 1.0, 6.0, ((0, 16), (1, 32)))
    out_grad = gaussian(key_of[3], (STREAM_POSITIONS, HEADS, VD), 0.05, 0.29882812, ((0, 16), (1, 32)))
    log_decay = draw_log_decay(jax.random.fold_in(key_of[10], 71), 0)
    start_state = gaussian(key_of[5], (GROUPS, HEADS, KD, VD), 4.0, 24.0, ((0, 16), (1, 32)), jnp.float32)
    layer_grad = gaussian(key_of[6], (STREAM_POSITIONS, D), 1.0, 6.0, ((0, 512),))
    gate_weights = jnp.clip(0.1 + 0.9 * jax.random.uniform(key_of[7], (STREAM_POSITIONS, TOP), jnp.float32) ** block_levels(key_of[7], (STREAM_POSITIONS, TOP), ((0, 512),), -0.2, 0.2), 0.1, 1.0)
    routes_keys = jax.random.split(jax.random.fold_in(key_of[8], 1), STREAM_POSITIONS // ROWS_DEV)
    routes_turns = jax.random.permutation(jax.random.fold_in(key_of[8], 3), STREAM_POSITIONS // ROWS_DEV)
    routes = jax.vmap(lambda own, number: shared_out(jax.random.fold_in(key_of[8], 2), own, number, ROWS_DEV, EXPERTS, TOP, MOST, 2))(routes_keys, routes_turns).reshape((STREAM_POSITIONS, TOP))
    expert_down = gaussian(key_of[9], (EXPERTS, FW, D), D ** -0.5, 0.125, ((0, 32),))
    return {"query_heads": query_heads, "key_heads": key_heads, "value_heads": value_heads, "out_grad": out_grad, "log_decay": log_decay, "start_state": start_state, "layer_grad": layer_grad, "gate_weights": gate_weights, "routes": routes, "expert_down": expert_down}


BEST_MATMUL_MODE = lax.Precision.HIGHEST


def group_forward(items):
    queries, key_rows, value_row_list, gradient_rows, decays, initial = items

    def advance(running_state, item):
        query_t, key_step, value_step, gradient_step, decay_t = item
        running_state = jnp.exp(decay_t)[:, :, None] * running_state + key_step[:, :, None] * value_step[:, None, :]
        return running_state, jnp.einsum("oig,og->oi", running_state, gradient_step, precision=BEST_MATMUL_MODE)

    return lax.scan(advance, initial, (queries, key_rows, value_row_list, gradient_rows, decays))[1]


def retreat(adjoint_state, item):
    query_t, key_step, value_step, gradient_step, decay_t = item
    adjoint_state = adjoint_state + query_t[:, :, None] * gradient_step[:, None, :]
    key_portion = jnp.einsum("oig,og->oi", adjoint_state, value_step, precision=BEST_MATMUL_MODE)
    value_portion = jnp.einsum("yau,ya->yu", adjoint_state, key_step, precision=BEST_MATMUL_MODE)
    return jnp.exp(decay_t)[:, :, None] * adjoint_state, (key_portion, value_portion)


def by_group(array):
    return array.reshape((GROUPS, TOK_CTX) + array.shape[1:])


def slot_positions(block_routes):
    flat = block_routes.reshape(-1)
    indicator_matrix = (flat[:, None] == jnp.arange(EXPERTS, dtype=jnp.int32)[None, :]).astype(jnp.int32)
    before = jnp.cumsum(indicator_matrix, axis=0) - indicator_matrix
    return flat * MOST + jnp.sum(before * indicator_matrix, axis=1)


def reference(query_heads, key_heads, value_heads, out_grad, log_decay, start_state, layer_grad, gate_weights, routes, expert_down):
    queries = query_heads.astype(jnp.float32)
    key_rows = key_heads.astype(jnp.float32)
    value_row_list = value_heads.astype(jnp.float32)
    gradient_rows = out_grad.astype(jnp.float32)
    decays = log_decay.astype(jnp.float32)
    grouped = (by_group(queries), by_group(key_rows), by_group(value_row_list), by_group(gradient_rows), by_group(decays), start_state)
    query_grad = lax.map(group_forward, grouped).reshape(queries.shape)
    initial = jnp.zeros((HEADS, KD, VD), jnp.float32)
    unused, parts = lax.scan(retreat, initial, (queries, key_rows, value_row_list, gradient_rows, decays), reverse=True)
    key_grad, value_grad = parts

    down_wide = expert_down.astype(jnp.float32)
    row_blocks = layer_grad.reshape(GROUPS * SOURCES, ROWS_DEV, D)
    gate_blocks = gate_weights.reshape(GROUPS * SOURCES, ROWS_DEV, TOP)
    route_blocks = routes.reshape(GROUPS * SOURCES, ROWS_DEV, TOP)

    def expert_block(items):
        grad_block, gate_block, route_block = items
        scaled = (gate_block[:, :, None] * grad_block[:, None, :].astype(jnp.float32)).astype(jnp.bfloat16).reshape(ROWS_DEV * TOP, D)
        position = slot_positions(route_block)
        buffer = jnp.zeros((EXPERTS * MOST, D), jnp.bfloat16).at[position].set(scaled).reshape(EXPERTS, MOST, D)
        product = jnp.einsum("emd,efd->emf", buffer.astype(jnp.float32), down_wide, precision=BEST_MATMUL_MODE)
        return product.astype(jnp.bfloat16)

    hidden_grad = lax.map(expert_block, (row_blocks, gate_blocks, route_blocks)).reshape(GROUPS, SOURCES, EXPERTS, MOST, FW)
    return (query_grad.astype(jnp.bfloat16), key_grad.astype(jnp.bfloat16), value_grad.astype(jnp.bfloat16), hidden_grad)
```

```python
import jax
import jax.numpy as jnp
from jax import lax
from jax.experimental import pallas as pl
from jax.experimental.pallas import tpu as pltpu
from jax.sharding import PartitionSpec as P

EXPERTS = 32
MOST = 16
ROWS = 32
CHUNK = 128
EXTRA = 128
F32 = jnp.float32
BF16 = jnp.bfloat16
NN = (((1,), (0,)), ((), ()))
NT = (((1,), (1,)), ((), ()))
TN = (((0,), (0,)), ((), ()))


def dot(left, right, dims=NN):
    return lax.dot_general(left, right, dims, preferred_element_type=F32)


def call(body, outs, operands, smem=0, hbm=0, scratch=()):
    spaces = [pltpu.SMEM] * smem + [pltpu.HBM] * hbm
    spaces += [pltpu.VMEM] * (len(operands) - len(spaces))
    return pl.pallas_call(
        body,
        out_shape=outs,
        in_specs=[pl.BlockSpec(memory_space=space) for space in spaces],
        out_specs=jax.tree.map(lambda _: pl.BlockSpec(memory_space=pltpu.VMEM), outs),
        scratch_shapes=scratch,
        compiler_params=pltpu.CompilerParams(vmem_limit_bytes=32 * 1024 * 1024),
        cost_estimate=pl.CostEstimate(flops=1000, bytes_accessed=1000, transcendentals=0),
    )(*operands)


def lower_mask():
    rows = lax.broadcasted_iota(jnp.int32, (CHUNK, CHUNK), 0)
    columns = lax.broadcasted_iota(jnp.int32, (CHUNK, CHUNK), 1)
    return rows >= columns


def pack_body(rows_ref, gates_ref, routes_ref, out_ref, gates_here, routes_here, sems):
    width = rows_ref.shape[1]
    copies = [
        pltpu.make_async_copy(gates_ref, gates_here, sems.at[0]),
        pltpu.make_async_copy(routes_ref, routes_here, sems.at[1]),
        pltpu.make_async_copy(rows_ref, out_ref.at[:, pl.ds(0, width)], sems.at[2]),
    ]
    for copy in copies:
        copy.start()
    lanes = lax.broadcasted_iota(jnp.int32, (ROWS, EXTRA), 1)
    dense = jnp.zeros((ROWS, EXTRA), F32)
    copies[0].wait()
    copies[1].wait()
    gates, routes = gates_here[...].T, routes_here[...].T
    for r in range(gates.shape[1]):
        hit = (lanes % EXPERTS) == routes[:, r : r + 1]
        dense = jnp.where(hit, gates[:, r : r + 1], dense)
    high = dense.astype(BF16).astype(F32)
    both = jnp.where(lanes < EXPERTS, high, jnp.where(lanes < 2 * EXPERTS, dense - high, 0.0))
    out_ref[:, width:] = both.astype(BF16)
    copies[2].wait()


def message_body(q_ref, g_ref, d_ref, out_ref):
    lower = lower_mask().astype(BF16)
    total = jnp.zeros((1, q_ref.shape[1]), F32)
    message = jnp.zeros((g_ref.shape[1], q_ref.shape[1]), F32)
    for n in range(q_ref.shape[0] // CHUNK):
        part = pl.ds(n * CHUNK, CHUNK)
        sums = dot(lower, d_ref[part]) + total
        total = sums[CHUNK - 1 :]
        scaled = (q_ref[part].astype(F32) * jnp.exp(sums)).astype(BF16)
        message += dot(g_ref[part], scaled, TN)
    out_ref[: message.shape[0]] = message
    out_ref[message.shape[0] :] = jnp.broadcast_to(jnp.exp(total), (8, total.shape[1]))


def heads_body(
    q_ref, k_ref, v_ref, g_ref, d_ref, start_ref, qg_ref, pk_ref, pv_ref, tail_ref, add_ref
):
    count = q_ref.shape[0] // CHUNK
    keep = lower_mask()
    lower = keep.astype(BF16)
    state = start_ref[...].T
    ends = []
    for n in range(count):
        part = pl.ds(n * CHUNK, CHUNK)
        queries, keys = q_ref[part].astype(F32), k_ref[part].astype(F32)
        values, grads = v_ref[part], g_ref[part]
        sums = dot(lower, d_ref[part])
        end, middle = sums[CHUNK - 1 :], sums[CHUNK // 2 - 1 : CHUNK // 2]
        ends.append(end)
        grow, shrink = jnp.exp(sums - middle), jnp.exp(middle - sums)
        whole = jnp.exp(sums)
        trail = jnp.exp(end - sums)
        enlarged, reduced = (queries * grow).astype(BF16), (keys * shrink).astype(BF16)
        score = jnp.where(keep, dot(grads, values, NT), 0.0).astype(BF16)
        affinity = jnp.where(keep, dot(enlarged, reduced, NT), 0.0).astype(BF16)
        query_grad = whole * dot(grads, state.astype(BF16)) + grow * dot(score, reduced)
        qg_ref[part] = query_grad.astype(BF16)
        pk_ref[part] = shrink * dot(score, enlarged, TN)
        pv_ref[part] = dot(affinity, grads, TN)
        add_ref[n] = dot(grads, (queries * whole).astype(BF16), TN)
        state = state * jnp.exp(end) + dot(values, (keys * trail).astype(BF16), TN)
        tail_ref[part] = end - sums
    later = jnp.zeros_like(ends[0])
    adjoint = jnp.zeros_like(state)
    for n in reversed(range(count)):
        part = pl.ds(n * CHUNK, CHUNK)
        left = tail_ref[part]
        if n < count - 1:
            trail = jnp.exp(left)
            arrived = adjoint.astype(BF16)
            pk_ref[part] += trail * dot(v_ref[part], arrived)
            scaled = (k_ref[part].astype(F32) * trail).astype(BF16)
            pv_ref[part] += dot(scaled, arrived, NT)
        tail_ref[part] = jnp.exp(left + later)
        later = later + ends[n]
        adjoint = add_ref[n] + jnp.exp(ends[n]) * adjoint


def arrival_body(k_ref, v_ref, in_ref, pk_ref, pv_ref, tail_ref, kg_ref, vg_ref):
    arrived = in_ref[: v_ref.shape[1]].astype(BF16)
    tail = tail_ref[...]
    kg_ref[...] = (pk_ref[...] + tail * dot(v_ref[...], arrived)).astype(BF16)
    scaled = (k_ref[...].astype(F32) * tail).astype(BF16)
    vg_ref[...] = (pv_ref[...] + dot(scaled, arrived, NT)).astype(BF16)


def slots(expert, rows_ref, down_ref, store):
    width = down_ref.shape[1]
    hidden = dot(rows_ref[:, :width], down_ref[...], NT)
    blocks = rows_ref.shape[0] // ROWS
    for first in range(0, blocks, 4):
        number = min(4, blocks - first)
        size = number * ROWS
        part = slice(first * ROWS, first * ROWS + size)
        gates = rows_ref[part, width:].astype(F32)
        lanes = lax.broadcasted_iota(jnp.int32, (size, EXTRA), 1)
        row = lax.broadcasted_iota(jnp.int32, (size, EXTRA), 0)
        high = jnp.sum(jnp.where(lanes == expert, gates, 0.0), axis=1, keepdims=True)
        low = jnp.sum(jnp.where(lanes == expert + EXPERTS, gates, 0.0), axis=1, keepdims=True)
        taken = jnp.broadcast_to(high > 0.0, (size, EXTRA))
        square = lax.broadcasted_iota(jnp.int32, (size, size), 0)
        across = lax.broadcasted_iota(jnp.int32, (size, size), 1)
        earlier = ((square > across) & (square // ROWS == across // ROWS)).astype(BF16)
        place = dot(earlier, taken.astype(BF16)).astype(jnp.int32) + (row // ROWS) * MOST
        hit = taken & (place == lanes)
        high = jnp.where(hit, high, 0.0).astype(BF16)
        low = jnp.where(hit, low, 0.0).astype(BF16)
        block = hidden[part]
        upper = block.astype(BF16)
        lower = (block - upper.astype(F32)).astype(BF16)
        result = dot(high, upper, TN) + dot(high, lower, TN) + dot(low, upper, TN)
        result = result.astype(BF16)
        for b in range(number):
            store(first + b, result[b * MOST : (b + 1) * MOST])


def hidden_body(me_ref, rows_ref, down_ref, out_ref):
    def store(block, result):
        out_ref[block * MOST : (block + 1) * MOST] = result

    slots(me_ref[0], rows_ref, down_ref, store)


def sender(me, hops, other, sibling):
    core = (me % 2 + sibling) % 2
    chip = (me // 2 + EXPERTS // 2 + (2 * core - 1) * hops) % (EXPERTS // 2)
    return chip * 2 + (core + other) % 2


def last_body(me_ref, done_ref, mine_ref, theirs_ref, down_ref, out_ref, rows_ref):
    me = me_ref[0]
    here = [(hops, other, 0) for hops in range(1, 5) for other in (0, 1)]
    blocks = [(0, 0, 0), (0, 1, 0), *here, *((h, o, 1) for h, o, _ in here)]
    for i, block in enumerate(blocks):
        out_ref[sender(me, *block)] = done_ref[i * MOST : (i + 1) * MOST]
    here = [*((hops, other, 0) for hops in (5, 6, 7) for other in (0, 1)), (8, 0, 0)]
    blocks = [*here, *((h, o, 1) for h, o, _ in here)]
    half = mine_ref.shape[0]
    rows_ref[:half] = mine_ref[...]
    rows_ref[half:] = theirs_ref[...]

    def store(i, result):
        out_ref[sender(me, *blocks[i])] = result

    slots(me, rows_ref, down_ref, store)


def move(array, hops):
    chips = EXPERTS // 2
    pairs = []
    for chip in range(chips):
        for core in range(2):
            step = hops if core == 0 else -hops
            pairs.append((2 * chip + core, 2 * ((chip + step) % chips) + core))
    return lax.ppermute(array, "exp", pairs)


def swap(array):
    return lax.ppermute(array, "exp", [(i, i ^ 1) for i in range(EXPERTS)])


def from_later(array, by):
    peers = lax.axis_size("ctx")
    return lax.ppermute(array, "ctx", [(i + by, i) for i in range(peers - by)])


def after(array, *others):
    return lax.optimization_barrier((array, *others))[0]


def combine(first, second, states):
    decay = first[states : states + 1]
    own = jnp.where(lax.broadcasted_iota(jnp.int32, first.shape, 0) < states, first, 0.0)
    return own + decay * second


def join_body(*refs):
    *parts, out_ref = refs
    first = 0
    for part in parts:
        out_ref[first : first + part.shape[0]] = part[...]
        first += part.shape[0]


def join(*parts):
    rows = sum(part.shape[0] for part in parts)
    out = jax.ShapeDtypeStruct((rows, parts[0].shape[1]), BF16)
    return call(join_body, out, parts)


def local(
    query_heads,
    key_heads,
    value_heads,
    out_grad,
    log_decay,
    start_state,
    layer_grad,
    gate_weights,
    routes,
    expert_down,
):
    length, _, kd = query_heads.shape
    vd = value_heads.shape[2]
    width = layer_grad.shape[1]
    hidden_width = expert_down.shape[1]
    queries, keys = query_heads.reshape(length, kd), key_heads.reshape(length, kd)
    values, grads = value_heads.reshape(length, vd), out_grad.reshape(length, vd)
    decays = log_decay.reshape(length, kd)
    down = expert_down.reshape(hidden_width, width)
    queries, keys, values, grads, decays, layer_grad, gates, chosen, start = (
        pltpu.with_memory_space_constraint(x, pltpu.HBM)
        for x in (
            queries,
            keys,
            values,
            grads,
            decays,
            layer_grad,
            gate_weights.T,
            routes.T,
            start_state.reshape(kd, vd),
        )
    )
    me = lax.axis_index("exp").astype(jnp.int32).reshape(1)
    struct = jax.ShapeDtypeStruct

    def hidden(array):
        return call(
            hidden_body,
            struct((array.shape[0] // ROWS * MOST, hidden_width), BF16),
            (me, array, down),
            smem=1,
        )

    with jax.named_scope("pack"):
        rows = call(
            pack_body,
            struct((ROWS, width + EXTRA), BF16),
            (layer_grad, gates, chosen),
            hbm=3,
            scratch=(
                pltpu.VMEM(gates.shape, F32),
                pltpu.VMEM(chosen.shape, jnp.int32),
                pltpu.SemaphoreType.DMA((3,)),
            ),
        )
    with jax.named_scope("message"):
        message = call(
            message_body, struct((vd + 8, kd), F32), (queries, grads, decays)
        )
    theirs = after(swap(rows), message)
    both = join(rows, theirs)
    with jax.named_scope("heads"):
        query_grad, key_part, value_part, tail = call(
            heads_body,
            (
                struct((length, kd), BF16),
                struct((length, kd), F32),
                struct((length, vd), F32),
                struct((length, kd), F32),
            ),
            (queries, keys, values, grads, decays, after(start, both)),
            scratch=(pltpu.VMEM((length // CHUNK, vd, kd), F32),),
        )

    rows1, rows2 = move(both, 1), move(both, 2)
    incoming = after(from_later(after(message, both), 1), rows1)
    within = combine(message, incoming, vd)
    rows3 = move(after(rows1, within, key_part), 2)
    rows4 = move(rows2, 2)
    incoming = combine(incoming, after(from_later(within, 2), rows3), vd)
    within = combine(message, incoming, vd)
    rows5 = move(after(rows3, within), 2)
    rows6 = move(rows4, 2)
    incoming = combine(incoming, after(from_later(within, 4), rows5), vd)
    within = combine(message, incoming, vd)
    rows7 = move(rows5, 2)
    with jax.named_scope("experts"):
        early = join(rows1, rows2, rows3, after(rows4, rows5))
        done = hidden(join(both, early, swap(early)))
    rows8 = move(after(rows6, within, done)[:ROWS], 2)
    incoming = combine(incoming, from_later(within, 8), vd)

    with jax.named_scope("arrival"):
        key_grad, value_grad = call(
            arrival_body,
            (struct((length, kd), BF16), struct((length, vd), BF16)),
            (keys, values, incoming, key_part, value_part, tail),
        )

    with jax.named_scope("experts"):
        late = after(join(rows5, rows6, rows7, rows8), incoming)
        hidden_grad = call(
            last_body,
            struct((EXPERTS, MOST, hidden_width), BF16),
            (me, done, late, swap(late), down),
            smem=1,
            scratch=(pltpu.VMEM((2 * late.shape[0], late.shape[1]), BF16),),
        )
    return (
        query_grad.reshape(length, 1, kd),
        key_grad.reshape(length, 1, kd),
        value_grad.reshape(length, 1, vd),
        hidden_grad.reshape(1, EXPERTS, 1, MOST, hidden_width),
    )


def solution(mesh):
    return jax.shard_map(
        local,
        mesh=mesh,
        in_specs=(
            P("ctx", "exp", None),
            P("ctx", "exp", None),
            P("ctx", "exp", None),
            P("ctx", "exp", None),
            P("ctx", "exp", None),
            P("ctx", "exp", None, None),
            P(("ctx", "exp"), None),
            P(("ctx", "exp"), None),
            P(("ctx", "exp"), None),
            P("exp", None, None),
        ),
        out_specs=(
            P("ctx", "exp", None),
            P("ctx", "exp", None),
            P("ctx", "exp", None),
            P("ctx", None, "exp", None, None),
        ),
        check_vma=False,
    )
```

```python
import jax
import jax.numpy as jnp
from jax import lax
from jax.experimental import pallas as pl
from jax.experimental.pallas import tpu as pltpu
from jax.sharding import PartitionSpec as P

EXPERTS = 32
MOST = 16
ROWS = 32
CHUNK = 128
EXTRA = 128
F32 = jnp.float32
BF16 = jnp.bfloat16
NN = (((1,), (0,)), ((), ()))
NT = (((1,), (1,)), ((), ()))
TN = (((0,), (0,)), ((), ()))


def dot(left, right, dims=NN):
    return lax.dot_general(left, right, dims, preferred_element_type=F32)


def call(body, outs, operands, smem=0, hbm=0, scratch=()):
    spaces = [pltpu.SMEM] * smem + [pltpu.HBM] * hbm
    spaces += [pltpu.VMEM] * (len(operands) - len(spaces))
    return pl.pallas_call(
        body,
        out_shape=outs,
        in_specs=[pl.BlockSpec(memory_space=space) for space in spaces],
        out_specs=jax.tree.map(lambda _: pl.BlockSpec(memory_space=pltpu.VMEM), outs),
        scratch_shapes=scratch,
        compiler_params=pltpu.CompilerParams(vmem_limit_bytes=32 * 1024 * 1024),
        cost_estimate=pl.CostEstimate(flops=1000, bytes_accessed=1000, transcendentals=0),
    )(*operands)


def lower_mask():
    rows = lax.broadcasted_iota(jnp.int32, (CHUNK, CHUNK), 0)
    columns = lax.broadcasted_iota(jnp.int32, (CHUNK, CHUNK), 1)
    return rows >= columns


def pack_body(rows_ref, gates_ref, routes_ref, out_ref, gates_here, routes_here, sems):
    width = rows_ref.shape[1]
    copies = [
        pltpu.make_async_copy(gates_ref, gates_here, sems.at[0]),
        pltpu.make_async_copy(routes_ref, routes_here, sems.at[1]),
        pltpu.make_async_copy(rows_ref, out_ref.at[:, pl.ds(0, width)], sems.at[2]),
    ]
    for copy in copies:
        copy.start()
    lanes = lax.broadcasted_iota(jnp.int32, (ROWS, EXTRA), 1)
    dense = jnp.zeros((ROWS, EXTRA), F32)
    copies[0].wait()
    copies[1].wait()
    gates, routes = gates_here[...].T, routes_here[...].T
    for r in range(gates.shape[1]):
        hit = (lanes % EXPERTS) == routes[:, r : r + 1]
        dense = jnp.where(hit, gates[:, r : r + 1], dense)
    high = dense.astype(BF16).astype(F32)
    both = jnp.where(lanes < EXPERTS, high, jnp.where(lanes < 2 * EXPERTS, dense - high, 0.0))
    out_ref[:, width:] = both.astype(BF16)
    copies[2].wait()


def message_body(q_ref, g_ref, d_ref, out_ref):
    lower = lower_mask().astype(BF16)
    total = jnp.zeros((1, q_ref.shape[1]), F32)
    message = jnp.zeros((g_ref.shape[1], q_ref.shape[1]), F32)
    for n in range(q_ref.shape[0] // CHUNK):
        part = pl.ds(n * CHUNK, CHUNK)
        sums = dot(lower, d_ref[part]) + total
        total = sums[CHUNK - 1 :]
        scaled = (q_ref[part].astype(F32) * jnp.exp(sums)).astype(BF16)
        message += dot(g_ref[part], scaled, TN)
    out_ref[: message.shape[0]] = message
    out_ref[message.shape[0] :] = jnp.broadcast_to(jnp.exp(total), (8, total.shape[1]))


def heads_body(
    q_ref, k_ref, v_ref, g_ref, d_ref, start_ref, qg_ref, pk_ref, pv_ref, tail_ref, add_ref
):
    count = q_ref.shape[0] // CHUNK
    keep = lower_mask()
    lower = keep.astype(BF16)
    state = start_ref[...].T
    ends = []
    for n in range(count):
        part = pl.ds(n * CHUNK, CHUNK)
        queries, keys = q_ref[part].astype(F32), k_ref[part].astype(F32)
        values, grads = v_ref[part], g_ref[part]
        sums = dot(lower, d_ref[part])
        end, middle = sums[CHUNK - 1 :], sums[CHUNK // 2 - 1 : CHUNK // 2]
        ends.append(end)
        grow, shrink = jnp.exp(sums - middle), jnp.exp(middle - sums)
        whole = jnp.exp(sums)
        trail = jnp.exp(end - sums)
        enlarged, reduced = (queries * grow).astype(BF16), (keys * shrink).astype(BF16)
        score = jnp.where(keep, dot(grads, values, NT), 0.0).astype(BF16)
        affinity = jnp.where(keep, dot(enlarged, reduced, NT), 0.0).astype(BF16)
        query_grad = whole * dot(grads, state.astype(BF16)) + grow * dot(score, reduced)
        qg_ref[part] = query_grad.astype(BF16)
        pk_ref[part] = shrink * dot(score, enlarged, TN)
        pv_ref[part] = dot(affinity, grads, TN)
        add_ref[n] = dot(grads, (queries * whole).astype(BF16), TN)
        state = state * jnp.exp(end) + dot(values, (keys * trail).astype(BF16), TN)
        tail_ref[part] = end - sums
    adjoint = jnp.zeros_like(state)
    for n in reversed(range(count)):
        part = pl.ds(n * CHUNK, CHUNK)
        left = tail_ref[part]
        if n < count - 1:
            trail = jnp.exp(left)
            arrived = adjoint.astype(BF16)
            pk_ref[part] += trail * dot(v_ref[part], arrived)
            scaled = (k_ref[part].astype(F32) * trail).astype(BF16)
            pv_ref[part] += dot(scaled, arrived, NT)
        adjoint = add_ref[n] + jnp.exp(ends[n]) * adjoint


def arrival_body(k_ref, v_ref, d_ref, in_ref, pk_ref, pv_ref, kg_ref, vg_ref):
    arrived = in_ref[: v_ref.shape[1]].astype(BF16)
    rows = lax.broadcasted_iota(jnp.int32, (CHUNK, CHUNK), 0)
    columns = lax.broadcasted_iota(jnp.int32, (CHUNK, CHUNK), 1)
    upper = (columns > rows).astype(BF16)
    later = jnp.zeros((1, k_ref.shape[1]), F32)
    for n in reversed(range(k_ref.shape[0] // CHUNK)):
        part = pl.ds(n * CHUNK, CHUNK)
        left = dot(upper, d_ref[part]) + later
        later = left[:1] + d_ref[part][:1].astype(F32)
        tail = jnp.exp(left)
        kg_ref[part] = (pk_ref[part] + tail * dot(v_ref[part], arrived)).astype(BF16)
        scaled = (k_ref[part].astype(F32) * tail).astype(BF16)
        vg_ref[part] = (pv_ref[part] + dot(scaled, arrived, NT)).astype(BF16)


def slots(expert, rows_ref, down_ref, store):
    width = down_ref.shape[1]
    hidden = dot(rows_ref[:, :width], down_ref[...], NT)
    blocks = rows_ref.shape[0] // ROWS
    for first in range(0, blocks, 4):
        number = min(4, blocks - first)
        size = number * ROWS
        part = slice(first * ROWS, first * ROWS + size)
        gates = rows_ref[part, width:].astype(F32)
        lanes = lax.broadcasted_iota(jnp.int32, (size, EXTRA), 1)
        row = lax.broadcasted_iota(jnp.int32, (size, EXTRA), 0)
        high = jnp.sum(jnp.where(lanes == expert, gates, 0.0), axis=1, keepdims=True)
        low = jnp.sum(jnp.where(lanes == expert + EXPERTS, gates, 0.0), axis=1, keepdims=True)
        taken = jnp.broadcast_to(high > 0.0, (size, EXTRA))
        square = lax.broadcasted_iota(jnp.int32, (size, size), 0)
        across = lax.broadcasted_iota(jnp.int32, (size, size), 1)
        earlier = ((square > across) & (square // ROWS == across // ROWS)).astype(BF16)
        place = dot(earlier, taken.astype(BF16)).astype(jnp.int32) + (row // ROWS) * MOST
        hit = taken & (place == lanes)
        high = jnp.where(hit, high, 0.0).astype(BF16)
        low = jnp.where(hit, low, 0.0).astype(BF16)
        block = hidden[part]
        upper = block.astype(BF16)
        result = dot(high, upper, TN) + dot(low, upper, TN)
        result = result.astype(BF16)
        for b in range(number):
            store(first + b, result[b * MOST : (b + 1) * MOST])


def hidden_body(me_ref, *refs, first=0):
    *parts, mine_ref, theirs_ref, own_ref, other_ref, rows_ref = refs
    row = 0
    for part in parts:
        rows_ref[row : row + part.shape[0]] = part[...]
        row += part.shape[0]
    for turn, (down_ref, out_ref) in enumerate(((mine_ref, own_ref), (theirs_ref, other_ref))):

        def store(block, result, out_ref=out_ref):
            out_ref[first + block * MOST : first + (block + 1) * MOST] = result

        slots(me_ref[0] ^ turn, rows_ref, down_ref, store)


def last_body(me_ref, own_done, other_done, *refs):
    *_, own_ref, other_ref, _ = refs
    first = own_done.shape[0]
    own_ref[:first] = own_done[...]
    other_ref[:first] = other_done[...]
    hidden_body(me_ref, *refs, first=first)


BLOCKS = ((0, 0), *((hops, other) for hops in range(1, 8) for other in range(2)), (8, 0))


def sender(me, block, sibling):
    hops, other = block
    core = (me % 2 + sibling) % 2
    chip = (me // 2 + EXPERTS // 2 + (2 * core - 1) * hops) % (EXPERTS // 2)
    return chip * 2 + (core + other) % 2


def place_body(me_ref, mine_ref, theirs_ref, out_ref):
    for sibling, ref in ((0, mine_ref), (1, theirs_ref)):
        for i, block in enumerate(BLOCKS):
            out_ref[sender(me_ref[0], block, sibling)] = ref[i * MOST : (i + 1) * MOST]


def move(array, hops):
    chips = EXPERTS // 2
    pairs = []
    for chip in range(chips):
        for core in range(2):
            step = hops if core == 0 else -hops
            pairs.append((2 * chip + core, 2 * ((chip + step) % chips) + core))
    return lax.ppermute(array, "exp", pairs)


def swap(array):
    return lax.ppermute(array, "exp", [(i, i ^ 1) for i in range(EXPERTS)])


def from_later(array, by):
    peers = lax.axis_size("ctx")
    return lax.ppermute(array, "ctx", [(i + by, i) for i in range(peers - by)])


def after(array, *others):
    return lax.optimization_barrier((array, *others))[0]


def combine(first, second, states):
    decay = first[states : states + 1]
    own = jnp.where(lax.broadcasted_iota(jnp.int32, first.shape, 0) < states, first, 0.0)
    return own + decay * second


def join_body(*refs):
    *parts, out_ref = refs
    first = 0
    for part in parts:
        out_ref[first : first + part.shape[0]] = part[...]
        first += part.shape[0]


def join(*parts):
    rows = sum(part.shape[0] for part in parts)
    out = jax.ShapeDtypeStruct((rows, parts[0].shape[1]), BF16)
    return call(join_body, out, parts)


def local(
    query_heads,
    key_heads,
    value_heads,
    out_grad,
    log_decay,
    start_state,
    layer_grad,
    gate_weights,
    routes,
    expert_down,
):
    length, _, kd = query_heads.shape
    vd = value_heads.shape[2]
    width = layer_grad.shape[1]
    hidden_width = expert_down.shape[1]
    queries, keys = query_heads.reshape(length, kd), key_heads.reshape(length, kd)
    values, grads = value_heads.reshape(length, vd), out_grad.reshape(length, vd)
    decays = log_decay.reshape(length, kd)
    down = expert_down.reshape(hidden_width, width)
    queries, keys, values, grads, decays, layer_grad, gates, chosen, start = (
        pltpu.with_memory_space_constraint(x, pltpu.HBM)
        for x in (
            queries,
            keys,
            values,
            grads,
            decays,
            layer_grad,
            gate_weights.T,
            routes.T,
            start_state.reshape(kd, vd),
        )
    )
    me = lax.axis_index("exp").astype(jnp.int32).reshape(1)
    struct = jax.ShapeDtypeStruct

    def hidden(body, *parts, done=()):
        size = sum(part.shape[0] for part in parts)
        slots_out = struct(
            (size // ROWS * MOST + sum(part.shape[0] for part in done[:1]), hidden_width), BF16
        )
        return call(
            body,
            (slots_out, slots_out),
            (me, *done, *parts, down, down_theirs),
            smem=1,
            scratch=(pltpu.VMEM((size, parts[0].shape[1]), BF16),),
        )

    with jax.named_scope("pack"):
        rows = call(
            pack_body,
            struct((ROWS, width + EXTRA), BF16),
            (layer_grad, gates, chosen),
            hbm=3,
            scratch=(
                pltpu.VMEM(gates.shape, F32),
                pltpu.VMEM(chosen.shape, jnp.int32),
                pltpu.SemaphoreType.DMA((3,)),
            ),
        )
    with jax.named_scope("message"):
        message = call(
            message_body, struct((vd + 8, kd), F32), (queries, grads, decays)
        )
    theirs = after(swap(rows), message)
    both = join(rows, theirs)
    down_theirs = swap(down)
    with jax.named_scope("heads"):
        query_grad, key_part, value_part = call(
            heads_body,
            (
                struct((length, kd), BF16),
                struct((length, kd), F32),
                struct((length, vd), F32),
            ),
            (queries, keys, values, grads, decays, after(start, both)),
            scratch=(pltpu.VMEM((length, kd), F32), pltpu.VMEM((length // CHUNK, vd, kd), F32)),
        )

    rows1, rows2 = move(both, 1), move(both, 2)
    incoming = after(from_later(after(message, both), 1), rows1)
    within = combine(message, incoming, vd)
    rows3 = move(after(rows1, key_part), 2)
    rows4 = move(after(rows2, within), 2)
    incoming = combine(incoming, after(from_later(within, 2), rows3), vd)
    within = combine(message, incoming, vd)
    rows5 = move(after(rows3, within), 2)
    rows6 = move(rows4, 2)
    incoming = combine(incoming, after(from_later(within, 4), rows5), vd)
    within = combine(message, incoming, vd)
    rows7 = move(rows5, 2)
    with jax.named_scope("experts"):
        done = hidden(hidden_body, rows, rows1, rows2, rows3, rows4, rows5, rows6)
    rows8 = move(after(rows6, within)[:ROWS], 2)
    incoming = combine(incoming, after(from_later(within, 8), *done), vd)

    with jax.named_scope("arrival"):
        key_grad, value_grad = call(
            arrival_body,
            (struct((length, kd), BF16), struct((length, vd), BF16)),
            (keys, values, decays, incoming, key_part, value_part),
        )

    with jax.named_scope("experts"):
        last = after(rows8, incoming)
        mine, theirs = hidden(last_body, rows7, last, done=done)
        hidden_grad = call(
            place_body,
            struct((EXPERTS, MOST, hidden_width), BF16),
            (me, mine, swap(theirs)),
            smem=1,
        )
    return (
        query_grad.reshape(length, 1, kd),
        key_grad.reshape(length, 1, kd),
        value_grad.reshape(length, 1, vd),
        hidden_grad.reshape(1, EXPERTS, 1, MOST, hidden_width),
    )


def solution(mesh):
    return jax.shard_map(
        local,
        mesh=mesh,
        in_specs=(
            P("ctx", "exp", None),
            P("ctx", "exp", None),
            P("ctx", "exp", None),
            P("ctx", "exp", None),
            P("ctx", "exp", None),
            P("ctx", "exp", None, None),
            P(("ctx", "exp"), None),
            P(("ctx", "exp"), None),
            P(("ctx", "exp"), None),
            P("exp", None, None),
        ),
        out_specs=(
            P("ctx", "exp", None),
            P("ctx", "exp", None),
            P("ctx", "exp", None),
            P("ctx", None, "exp", None, None),
        ),
        check_vma=False,
    )
```

```python
import jax
import jax.numpy as jnp
from jax import lax
from jax.experimental import pallas as pl
from jax.experimental.pallas import tpu as pltpu
from jax.sharding import PartitionSpec as P

EXPERTS = 32
MOST = 16
ROWS = 32
CHUNK = 128
EXTRA = 128
F32 = jnp.float32
BF16 = jnp.bfloat16
NN = (((1,), (0,)), ((), ()))
NT = (((1,), (1,)), ((), ()))
TN = (((0,), (0,)), ((), ()))


def dot(left, right, dims=NN):
    return lax.dot_general(left, right, dims, preferred_element_type=F32)


def call(body, outs, operands, smem=0, hbm=0, scratch=()):
    spaces = [pltpu.SMEM] * smem + [pltpu.HBM] * hbm
    spaces += [pltpu.VMEM] * (len(operands) - len(spaces))
    return pl.pallas_call(
        body,
        out_shape=outs,
        in_specs=[pl.BlockSpec(memory_space=space) for space in spaces],
        out_specs=jax.tree.map(lambda _: pl.BlockSpec(memory_space=pltpu.VMEM), outs),
        scratch_shapes=scratch,
        compiler_params=pltpu.CompilerParams(vmem_limit_bytes=32 * 1024 * 1024),
        cost_estimate=pl.CostEstimate(flops=1000, bytes_accessed=1000, transcendentals=0),
    )(*operands)


def lower_mask():
    rows = lax.broadcasted_iota(jnp.int32, (CHUNK, CHUNK), 0)
    columns = lax.broadcasted_iota(jnp.int32, (CHUNK, CHUNK), 1)
    return rows >= columns


def pack_body(rows_ref, gates_ref, routes_ref, out_ref, gates_here, routes_here, sems):
    width = rows_ref.shape[1]
    copies = [
        pltpu.make_async_copy(gates_ref, gates_here, sems.at[0]),
        pltpu.make_async_copy(routes_ref, routes_here, sems.at[1]),
        pltpu.make_async_copy(rows_ref, out_ref.at[:, pl.ds(0, width)], sems.at[2]),
    ]
    for copy in copies:
        copy.start()
    lanes = lax.broadcasted_iota(jnp.int32, (ROWS, EXTRA), 1)
    dense = jnp.zeros((ROWS, EXTRA), F32)
    copies[0].wait()
    copies[1].wait()
    gates, routes = gates_here[...].T, routes_here[...].T
    for r in range(gates.shape[1]):
        hit = (lanes % EXPERTS) == routes[:, r : r + 1]
        dense = jnp.where(hit, gates[:, r : r + 1], dense)
    high = dense.astype(BF16).astype(F32)
    both = jnp.where(lanes < EXPERTS, high, jnp.where(lanes < 2 * EXPERTS, dense - high, 0.0))
    out_ref[:, width:] = both.astype(BF16)
    copies[2].wait()


def message_body(q_ref, g_ref, d_ref, out_ref):
    lower = lower_mask().astype(BF16)
    total = jnp.zeros((1, q_ref.shape[1]), F32)
    message = jnp.zeros((g_ref.shape[1], q_ref.shape[1]), F32)
    for n in range(q_ref.shape[0] // CHUNK):
        part = pl.ds(n * CHUNK, CHUNK)
        sums = dot(lower, d_ref[part]) + total
        total = sums[CHUNK - 1 :]
        scaled = (q_ref[part].astype(F32) * jnp.exp(sums)).astype(BF16)
        message += dot(g_ref[part], scaled, TN)
    out_ref[: message.shape[0]] = message
    out_ref[message.shape[0] :] = jnp.broadcast_to(jnp.exp(total), (8, total.shape[1]))


def heads_body(
    q_ref, k_ref, v_ref, g_ref, d_ref, start_ref, qg_ref, pk_ref, pv_ref, tail_ref, add_ref
):
    count = q_ref.shape[0] // CHUNK
    keep = lower_mask()
    lower = keep.astype(BF16)
    state = start_ref[...].T
    ends = []
    for n in range(count):
        part = pl.ds(n * CHUNK, CHUNK)
        queries, keys = q_ref[part].astype(F32), k_ref[part].astype(F32)
        values, grads = v_ref[part], g_ref[part]
        sums = dot(lower, d_ref[part])
        end, middle = sums[CHUNK - 1 :], sums[CHUNK // 2 - 1 : CHUNK // 2]
        ends.append(end)
        grow, shrink = jnp.exp(sums - middle), jnp.exp(middle - sums)
        whole = jnp.exp(sums)
        trail = jnp.exp(end - sums)
        enlarged, reduced = (queries * grow).astype(BF16), (keys * shrink).astype(BF16)
        score = jnp.where(keep, dot(grads, values, NT), 0.0).astype(BF16)
        affinity = jnp.where(keep, dot(enlarged, reduced, NT), 0.0).astype(BF16)
        query_grad = whole * dot(grads, state.astype(BF16)) + grow * dot(score, reduced)
        qg_ref[part] = query_grad.astype(BF16)
        pk_ref[part] = shrink * dot(score, enlarged, TN)
        pv_ref[part] = dot(affinity, grads, TN)
        add_ref[n] = dot(grads, (queries * whole).astype(BF16), TN)
        state = state * jnp.exp(end) + dot(values, (keys * trail).astype(BF16), TN)
        tail_ref[part] = end - sums
    adjoint = jnp.zeros_like(state)
    for n in reversed(range(count)):
        part = pl.ds(n * CHUNK, CHUNK)
        left = tail_ref[part]
        if n < count - 1:
            trail = jnp.exp(left)
            arrived = adjoint.astype(BF16)
            pk_ref[part] += trail * dot(v_ref[part], arrived)
            scaled = (k_ref[part].astype(F32) * trail).astype(BF16)
            pv_ref[part] += dot(scaled, arrived, NT)
        adjoint = add_ref[n] + jnp.exp(ends[n]) * adjoint


def arrival_body(k_ref, v_ref, d_ref, in_ref, pk_ref, pv_ref, kg_ref, vg_ref):
    arrived = in_ref[: v_ref.shape[1]].astype(BF16)
    rows = lax.broadcasted_iota(jnp.int32, (CHUNK, CHUNK), 0)
    columns = lax.broadcasted_iota(jnp.int32, (CHUNK, CHUNK), 1)
    upper = (columns > rows).astype(BF16)
    later = jnp.zeros((1, k_ref.shape[1]), F32)
    for n in reversed(range(k_ref.shape[0] // CHUNK)):
        part = pl.ds(n * CHUNK, CHUNK)
        left = dot(upper, d_ref[part]) + later
        later = left[:1] + d_ref[part][:1].astype(F32)
        tail = jnp.exp(left)
        kg_ref[part] = (pk_ref[part] + tail * dot(v_ref[part], arrived)).astype(BF16)
        scaled = (k_ref[part].astype(F32) * tail).astype(BF16)
        vg_ref[part] = (pv_ref[part] + dot(scaled, arrived, NT)).astype(BF16)


def slots(expert, rows_ref, down_ref, store):
    width = down_ref.shape[1]
    hidden = dot(rows_ref[:, :width], down_ref[...], NT)
    blocks = rows_ref.shape[0] // ROWS
    for first in range(0, blocks, 4):
        number = min(4, blocks - first)
        size = number * ROWS
        part = slice(first * ROWS, first * ROWS + size)
        gates = rows_ref[part, width:].astype(F32)
        lanes = lax.broadcasted_iota(jnp.int32, (size, EXTRA), 1)
        row = lax.broadcasted_iota(jnp.int32, (size, EXTRA), 0)
        high = jnp.sum(jnp.where(lanes == expert, gates, 0.0), axis=1, keepdims=True)
        low = jnp.sum(jnp.where(lanes == expert + EXPERTS, gates, 0.0), axis=1, keepdims=True)
        taken = jnp.broadcast_to(high > 0.0, (size, EXTRA))
        square = lax.broadcasted_iota(jnp.int32, (size, size), 0)
        across = lax.broadcasted_iota(jnp.int32, (size, size), 1)
        earlier = ((square > across) & (square // ROWS == across // ROWS)).astype(BF16)
        place = dot(earlier, taken.astype(BF16)).astype(jnp.int32) + (row // ROWS) * MOST
        hit = taken & (place == lanes)
        high = jnp.where(hit, high, 0.0).astype(BF16)
        low = jnp.where(hit, low, 0.0).astype(BF16)
        block = hidden[part]
        upper = block.astype(BF16)
        result = dot(jnp.concatenate([high, low]), jnp.concatenate([upper, upper]), TN)
        result = result.astype(BF16)
        for b in range(number):
            store(first + b, result[b * MOST : (b + 1) * MOST])


def hidden_body(me_ref, *refs, first=0):
    *parts, mine_ref, theirs_ref, own_ref, other_ref, rows_ref = refs
    row = 0
    for part in parts:
        rows_ref[row : row + part.shape[0]] = part[...]
        row += part.shape[0]
    for turn, (down_ref, out_ref) in enumerate(((mine_ref, own_ref), (theirs_ref, other_ref))):

        def store(block, result, out_ref=out_ref):
            out_ref[first + block * MOST : first + (block + 1) * MOST] = result

        slots(me_ref[0] ^ turn, rows_ref, down_ref, store)


def last_body(me_ref, own_done, other_done, *refs):
    *_, own_ref, other_ref, _ = refs
    first = own_done.shape[0]
    own_ref[:first] = own_done[...]
    other_ref[:first] = other_done[...]
    hidden_body(me_ref, *refs, first=first)


BLOCKS = ((0, 0), *((hops, other) for hops in range(1, 8) for other in range(2)), (8, 0))


def sender(me, block, sibling):
    hops, other = block
    core = (me % 2 + sibling) % 2
    chip = (me // 2 + EXPERTS // 2 + (2 * core - 1) * hops) % (EXPERTS // 2)
    return chip * 2 + (core + other) % 2


def place_body(me_ref, mine_ref, theirs_ref, out_ref):
    for sibling, ref in ((0, mine_ref), (1, theirs_ref)):
        for i, block in enumerate(BLOCKS):
            out_ref[sender(me_ref[0], block, sibling)] = ref[i * MOST : (i + 1) * MOST]


def move(array, hops):
    chips = EXPERTS // 2
    pairs = []
    for chip in range(chips):
        for core in range(2):
            step = hops if core == 0 else -hops
            pairs.append((2 * chip + core, 2 * ((chip + step) % chips) + core))
    return lax.ppermute(array, "exp", pairs)


def swap(array):
    return lax.ppermute(array, "exp", [(i, i ^ 1) for i in range(EXPERTS)])


def from_later(array, by):
    peers = lax.axis_size("ctx")
    return lax.ppermute(array, "ctx", [(i + by, i) for i in range(peers - by)])


def after(array, *others):
    return lax.optimization_barrier((array, *others))[0]


def combine(first, second, states):
    decay = first[states : states + 1]
    own = jnp.where(lax.broadcasted_iota(jnp.int32, first.shape, 0) < states, first, 0.0)
    return own + decay * second


def join_body(*refs):
    *parts, out_ref = refs
    first = 0
    for part in parts:
        out_ref[first : first + part.shape[0]] = part[...]
        first += part.shape[0]


def join(*parts):
    rows = sum(part.shape[0] for part in parts)
    out = jax.ShapeDtypeStruct((rows, parts[0].shape[1]), BF16)
    return call(join_body, out, parts)


def local(
    query_heads,
    key_heads,
    value_heads,
    out_grad,
    log_decay,
    start_state,
    layer_grad,
    gate_weights,
    routes,
    expert_down,
):
    length, _, kd = query_heads.shape
    vd = value_heads.shape[2]
    width = layer_grad.shape[1]
    hidden_width = expert_down.shape[1]
    queries, keys = query_heads.reshape(length, kd), key_heads.reshape(length, kd)
    values, grads = value_heads.reshape(length, vd), out_grad.reshape(length, vd)
    decays = log_decay.reshape(length, kd)
    down = expert_down.reshape(hidden_width, width)
    queries, keys, values, grads, decays, layer_grad, gates, chosen, start = (
        pltpu.with_memory_space_constraint(x, pltpu.HBM)
        for x in (
            queries,
            keys,
            values,
            grads,
            decays,
            layer_grad,
            gate_weights.T,
            routes.T,
            start_state.reshape(kd, vd),
        )
    )
    me = lax.axis_index("exp").astype(jnp.int32).reshape(1)
    struct = jax.ShapeDtypeStruct

    def hidden(body, *parts, done=()):
        size = sum(part.shape[0] for part in parts)
        slots_out = struct(
            (size // ROWS * MOST + sum(part.shape[0] for part in done[:1]), hidden_width), BF16
        )
        return call(
            body,
            (slots_out, slots_out),
            (me, *done, *parts, down, down_theirs),
            smem=1,
            scratch=(pltpu.VMEM((size, parts[0].shape[1]), BF16),),
        )

    with jax.named_scope("pack"):
        rows = call(
            pack_body,
            struct((ROWS, width + EXTRA), BF16),
            (layer_grad, gates, chosen),
            hbm=3,
            scratch=(
                pltpu.VMEM(gates.shape, F32),
                pltpu.VMEM(chosen.shape, jnp.int32),
                pltpu.SemaphoreType.DMA((3,)),
            ),
        )
    with jax.named_scope("message"):
        message = call(
            message_body, struct((vd + 8, kd), F32), (queries, grads, decays)
        )
    theirs = after(swap(rows), message)
    both = join(rows, theirs)
    down_theirs = swap(down)
    with jax.named_scope("heads"):
        query_grad, key_part, value_part = call(
            heads_body,
            (
                struct((length, kd), BF16),
                struct((length, kd), F32),
                struct((length, vd), F32),
            ),
            (queries, keys, values, grads, decays, after(start, both)),
            scratch=(pltpu.VMEM((length, kd), F32), pltpu.VMEM((length // CHUNK, vd, kd), F32)),
        )

    rows1, rows2 = move(both, 1), move(both, 2)
    incoming = after(from_later(after(message, both), 1), rows1)
    within = combine(message, incoming, vd)
    rows3 = move(after(rows1, key_part), 2)
    rows4 = move(after(rows2, within), 2)
    incoming = combine(incoming, after(from_later(within, 2), rows3), vd)
    within = combine(message, incoming, vd)
    rows5 = move(after(rows3, within), 2)
    rows6 = move(rows4, 2)
    incoming = combine(incoming, after(from_later(within, 4), rows5), vd)
    within = combine(message, incoming, vd)
    rows7 = move(rows5, 2)
    with jax.named_scope("experts"):
        done = hidden(hidden_body, rows, rows1, rows2, rows3, rows4, rows5, rows6)
    rows8 = move(after(rows6, within)[:ROWS], 2)
    incoming = combine(incoming, after(from_later(within, 8), *done), vd)

    with jax.named_scope("arrival"):
        key_grad, value_grad = call(
            arrival_body,
            (struct((length, kd), BF16), struct((length, vd), BF16)),
            (keys, values, decays, incoming, key_part, value_part),
        )

    with jax.named_scope("experts"):
        last = after(rows8, incoming)
        mine, theirs = hidden(last_body, rows7, last, done=done)
        hidden_grad = call(
            place_body,
            struct((EXPERTS, MOST, hidden_width), BF16),
            (me, mine, swap(theirs)),
            smem=1,
        )
    return (
        query_grad.reshape(length, 1, kd),
        key_grad.reshape(length, 1, kd),
        value_grad.reshape(length, 1, vd),
        hidden_grad.reshape(1, EXPERTS, 1, MOST, hidden_width),
    )


def solution(mesh):
    return jax.shard_map(
        local,
        mesh=mesh,
        in_specs=(
            P("ctx", "exp", None),
            P("ctx", "exp", None),
            P("ctx", "exp", None),
            P("ctx", "exp", None),
            P("ctx", "exp", None),
            P("ctx", "exp", None, None),
            P(("ctx", "exp"), None),
            P(("ctx", "exp"), None),
            P(("ctx", "exp"), None),
            P("exp", None, None),
        ),
        out_specs=(
            P("ctx", "exp", None),
            P("ctx", "exp", None),
            P("ctx", "exp", None),
            P("ctx", None, "exp", None, None),
        ),
        check_vma=False,
    )
```
